1024 devices in a mesh: row: 64 (over y, z_lo), col: 16 (over x, z_hi, core).
Axes of the slice: x: 4, y: 8, z: 16 (z_hi: 2, z_lo: 8; z = z_hi * 8 + z_lo), core: 2. Of those that a mesh axis runs over, the one named last changes fastest.
Arguments:
- vectors: bfloat16 [4096, 4, 256], P(('row', 'col')), may hold values from -6 to 6
- tiles: bfloat16 [64, 16, 6, 256, 256], P('row', 'col'), may hold values from -0.375 to 0.375
- tile_rows: int32 [64, 16, 6], P('row', 'col'), may hold values from 0 to 63, as said below
- tile_cols: int32 [64, 16, 6], P('row', 'col'), may hold values from 0 to 255
- tile_counts: int32 [64, 16], P('row', 'col'), may hold values from 1 to 6, as said below
Outputs:
- product: float32 [4096, 4, 256], P(('row', 'col'))
The draws below stay inside these ranges and needn't reach their ends.
Inputs may be any that keep to these rules, and one draw needn't show every extreme that they name: The first tile_counts slots of a grid position hold its live tiles. `tile_rows`: for every slot the global row block is not after the global column block.
All inputs are finite; a program needn't handle non-finite values.
Results may differ from the reference program's by a relative error of at most 0.00065.
Values may be sent and summed in bfloat16 or wider, within the bound.
A program may use at most 32 MiB of HBM per device.

```python
import jax
import jax.numpy as jnp
from jax import lax

NVEC = 4
TILE = 256
VB = 4
TPD = 6
GRID_ROWS = 64
GRID_COLS = 16
SLAB_BLK = 64
SEG_BLK = 256
NBLK = 4096


def tile_coords(key):
    shared = jax.random.fold_in(key, 5)
    row_key, col_key, pick_key, place_key = jax.random.split(shared, 4)
    grid_row = jnp.arange(GRID_ROWS, dtype=jnp.int32)[:, None, None]
    grid_col = jnp.arange(GRID_COLS, dtype=jnp.int32)[None, :, None]
    slot_order = jnp.arange(TPD, dtype=jnp.int32)[None, None, :]
    lowest = grid_row * VB
    reach = SEG_BLK - lowest
    raw_cols = jax.random.randint(col_key, (GRID_ROWS, GRID_COLS, TPD), 0, SEG_BLK, dtype=jnp.int32)
    columns = lowest + raw_cols % reach
    rows_raw = jax.random.randint(row_key, (GRID_ROWS, GRID_COLS, TPD), 0, SLAB_BLK, dtype=jnp.int32)
    at_top = (grid_row == 0) & (slot_order == 0)
    columns = jnp.where(at_top, SEG_BLK - 1, columns)
    chosen_row = jax.random.randint(pick_key, (), 0, GRID_ROWS - 1, dtype=jnp.int32)
    chosen_col = jax.random.randint(place_key, (), 0, GRID_COLS, dtype=jnp.int32)
    at_chosen = (grid_row == chosen_row) & (grid_col == chosen_col) & (slot_order == 0)
    columns = jnp.where(at_chosen, SEG_BLK - 1, columns)
    rows_raw = jnp.where(at_chosen, SLAB_BLK - 1, rows_raw)
    at_anchor = (grid_row == 0) & (grid_col == chosen_col) & (slot_order == 1)
    columns = jnp.where(at_anchor, 0, columns)
    rows_raw = jnp.where(at_anchor, 0, rows_raw)
    same_slab = columns // VB == grid_row
    ceiling = grid_col * VB + columns % VB
    rows_out = jnp.where(same_slab, jnp.minimum(rows_raw, ceiling), rows_raw)
    return (rows_out.astype(jnp.int32), columns.astype(jnp.int32))


def draw_tile_rows(key, part):
    coords = tile_coords(key)
    return coords[0]


def draw_tile_cols(key, part):
    coords = tile_coords(key)
    return coords[1]


def draw_tile_counts(key, part):
    key = jax.random.fold_in(key, 11)
    drop_key, full_key = jax.random.split(key, 2)
    grid_row = jnp.arange(GRID_ROWS, dtype=jnp.int32)[:, None]
    grid_col = jnp.arange(GRID_COLS, dtype=jnp.int32)[None, :]
    baseline = (TPD * (GRID_ROWS - grid_row) + GRID_ROWS - 1) // GRID_ROWS
    dropped = jax.random.randint(drop_key, (GRID_ROWS, GRID_COLS), 0, TPD // 4 + 1, dtype=jnp.int32)
    filled = jnp.clip(baseline - dropped, 1, TPD)
    full_col = jax.random.randint(full_key, (), 0, GRID_COLS, dtype=jnp.int32)
    filled = jnp.where((grid_row == 0) & (grid_col == full_col), TPD, filled)
    return filled.astype(jnp.int32)


def block_levels(key, extent, cuts, least, largest):
    def one(dim, parts):
        steps = jax.random.uniform(jax.random.fold_in(jax.random.fold_in(key, 6), dim), (parts,), jnp.float32, least / len(cuts), largest / len(cuts))
        return jnp.repeat(jnp.exp(steps), extent[dim] // parts).reshape((-1,) + (1,) * (len(extent) - dim - 1))

    loudness = one(*cuts[0])
    for cut in cuts[1:]:
        loudness = loudness * one(*cut)
    return loudness


def scatter_about(own_key, extent, deviation, limit, shards=(), kind=jnp.bfloat16):
    array = jax.random.normal(own_key, extent, jnp.float32) * deviation
    if len(shards) > 0:
        array = block_levels(own_key, extent, shards, -0.22, 0.18) * array
    return jnp.clip(array, min=-limit, max=limit).astype(kind)


def setup_inputs(seed: int = 0) -> dict:
    splits = jax.random.split(jax.random.key(seed), 6)
    vectors = scatter_about(splits[0], (NBLK, NVEC, TILE), 1.0, 6.0, ((0, 1024),))
    tiles = scatter_about(splits[1], (GRID_ROWS, GRID_COLS, TPD, TILE, TILE), TILE ** -0.5, 0.375, ((0, 64), (1, 16)))
    tile_rows = draw_tile_rows(jax.random.fold_in(splits[5], 71), 0)
    tile_cols = draw_tile_cols(jax.random.fold_in(splits[5], 71), 0)
    tile_counts = draw_tile_counts(jax.random.fold_in(splits[5], 71), 0)
    return {"vectors": vectors, "tiles": tiles, "tile_rows": tile_rows, "tile_cols": tile_cols, "tile_counts": tile_counts}


def reference(vectors, tiles, tile_rows, tile_cols, tile_counts):
    grid_total = GRID_ROWS * GRID_COLS
    slot_total = tile_rows.shape[2]
    flat_tiles = tiles.reshape((grid_total, slot_total, TILE, TILE))
    flat_rows = tile_rows.reshape((grid_total, slot_total))
    flat_cols = tile_cols.reshape((grid_total, slot_total))
    flat_filled = tile_counts.reshape((grid_total,))
    positions = jnp.arange(grid_total, dtype=jnp.int32)
    slot_order = jnp.arange(slot_total, dtype=jnp.int32)

    def one_position(running_sum, inputs):
        blocks, row_local, col_local, filled, position = inputs
        grid_row = position // GRID_COLS
        grid_col = position % GRID_COLS
        row_block = (grid_row * SLAB_BLK + row_local).astype(jnp.int32)
        column_block = (((col_local // VB) * GRID_COLS + grid_col) * VB + col_local % VB).astype(jnp.int32)
        live_mask = (slot_order < filled).astype(jnp.float32)[:, None, None]
        tile_values = blocks.astype(jnp.float32)
        column_vectors = vectors[column_block].astype(jnp.float32)
        row_vectors = vectors[row_block].astype(jnp.float32)
        to_rows = jnp.einsum("svk,sik->svi", column_vectors, tile_values, precision=lax.Precision.HIGHEST) * live_mask
        to_columns = jnp.einsum("svi,sik->svk", row_vectors, tile_values, precision=lax.Precision.HIGHEST) * live_mask
        running_sum = running_sum.at[row_block].add(to_rows)
        running_sum = running_sum.at[column_block].add(to_columns)
        return running_sum, None

    start_sum = jnp.zeros((NBLK, NVEC, TILE), jnp.float32)
    product, unused = lax.scan(one_position, start_sum, (flat_tiles, flat_rows, flat_cols, flat_filled, positions))
    return product
```

```python
import functools

import jax
import jax.numpy as jnp
from jax import lax
from jax.experimental import pallas as pl
from jax.experimental.pallas import tpu as pltpu
from jax.sharding import PartitionSpec as P

MESH = pl.DeviceIdType.MESH
NVEC = 4
TILE = 256
VB = 4
ROWS = VB * NVEC
PAD = 8
SLOT_ROWS = PAD * NVEC
LANES = 128
NONE = -(2**20)

H_VEC, G_CODE, Y_CODE, Z_VEC, G_VEC, Y_VEC, Y_PROD, G_PROD, Z_PROD, H_PROD = range(10)


def widen(row_of):
    sub = lax.broadcasted_iota(jnp.int32, (8, LANES), 0)
    pieces = []
    for k in range(PAD // 2):
        low = jnp.broadcast_to(row_of(2 * k), (8, LANES))
        high = jnp.broadcast_to(row_of(2 * k + 1), (8, LANES))
        pieces.append(jnp.where(sub < 4, low, high) + (sub & 3))
    return jnp.concatenate(pieces, axis=0)


def onehot(codes, base):
    lane = lax.broadcasted_iota(jnp.int32, codes.shape, 1)
    return jnp.where(codes == lane + base, 1.0, 0.0).astype(jnp.float32)


def place(matrix, products):
    high = products.astype(jnp.bfloat16)
    low = (products - high.astype(jnp.float32)).astype(jnp.bfloat16)
    return jnp.dot(matrix, high, preferred_element_type=jnp.float32) + jnp.dot(
        matrix, low, preferred_element_type=jnp.float32
    )


def kernel(
    sizes,
    vec_hbm, tiles_hbm, rows_hbm, cols_hbm, counts_hbm,
    out_ref,
    vin, tiles, rows_s, cols_s, counts_s,
    vz, vh, vg, ccode, rcode, ysend, yrecv, cprod, rprod, zsend, zrecv, hsend, hrecv,
    local_sem, send_sem, recv_sem,
):
    ny, nz, nx, nh, nc = sizes
    ng = nx * nc
    slots = tiles.shape[0]
    live_rows = slots * NVEC
    row, col = lax.axis_index("row"), lax.axis_index("col")
    y, z = row // nz, row % nz
    x, h, c = col // (nh * nc), (col // nc) % nh, col % nc
    g = x * nc + c

    def at(y_, z_, x_, h_, c_):
        return (y_ * nz + z_, (x_ * nh + h_) * nc + c_)

    def y_peer(k):
        p = lax.rem(y + k, ny)
        return p, at(p, z, x, h, c)

    def z_peer(k):
        p = lax.rem(z + k, nz)
        return p, at(y, p, x, h, c)

    def g_peer(k):
        p = lax.rem(g + k, ng)
        return p, at(y, z, p // nc, h, lax.rem(p, nc))

    h_other = nh - 1 - h
    h_id = at(y, z, x, h_other, c)
    groups = ((y_peer, ny), (z_peer, nz), (g_peer, ng))

    barrier = pltpu.get_barrier_semaphore()
    for peer, n in groups:
        @pl.loop(1, n)
        def _(k, peer=peer):
            pl.semaphore_signal(barrier, inc=1, device_id=peer(k)[1], device_id_type=MESH)
    pl.semaphore_signal(barrier, inc=1, device_id=h_id, device_id_type=MESH)

    locals_ = [
        pltpu.make_async_copy(src, dst, local_sem.at[i])
        for i, (src, dst) in enumerate(
            (
                (vec_hbm, vin),
                (rows_hbm, rows_s),
                (cols_hbm, cols_s),
                (counts_hbm, counts_s),
                (tiles_hbm.at[0, 0], tiles),
            )
        )
    ]
    for copy in locals_:
        copy.start()

    def send(which, src, dst, device_id):
        pltpu.make_async_remote_copy(
            src_ref=src,
            dst_ref=dst,
            send_sem=send_sem.at[which],
            recv_sem=recv_sem.at[which],
            device_id=device_id,
            device_id_type=MESH,
        ).start()

    def wait(sem, ref):
        pltpu.make_async_copy(ref, ref, sem).wait()

    def send_all(which, peer, n, src_of, dst):
        @pl.loop(1, n)
        def _(k):
            p, device_id = peer(k)
            send(which, src_of(p), dst, device_id)

    tail = SLOT_ROWS - live_rows
    if tail:
        cprod[:, live_rows:, :] = jnp.zeros((ny, tail, TILE), jnp.float32)
        rprod[:, live_rows:, :] = jnp.zeros((ng, tail, TILE), jnp.float32)

    locals_[0].wait()
    own = jnp.concatenate([vin[j].astype(jnp.float32) for j in range(VB)], axis=0)
    own = own.astype(jnp.bfloat16)
    vz[z] = own
    vh[h] = own
    for i in (1, 2, 3):
        locals_[i].wait()
    live = counts_s[0, 0]
    sub = lax.broadcasted_iota(jnp.int32, (PAD, LANES), 0)
    col_codes = jnp.full((PAD, LANES), NONE, jnp.int32)
    row_codes = col_codes
    for s in range(slots):
        q = cols_s[0, 0, s]
        p = rows_s[0, 0, s]
        owner, block = p // VB, p % VB
        px, ph, pc = owner // (nh * nc), (owner // nc) % nh, owner % nc
        place_at = ((px * nc + pc) * nh + ph) * ROWS + block * NVEC
        col_codes = jnp.where(sub == s, jnp.where(s < live, q * NVEC, NONE), col_codes)
        row_codes = jnp.where(sub == s, jnp.where(s < live, place_at, NONE), row_codes)
    ccode[y] = col_codes
    rcode[g] = row_codes

    pl.semaphore_wait(barrier, ny + nz + ng - 3 + 1)

    send(H_VEC, vh.at[h], vh.at[h], h_id)
    send_all(G_CODE, g_peer, ng, lambda p: rcode.at[g], rcode.at[g])
    send_all(Y_CODE, y_peer, ny, lambda p: ccode.at[y], ccode.at[y])
    send_all(Z_VEC, z_peer, nz, lambda p: vz.at[z], vz.at[z])

    wait(recv_sem.at[H_VEC], hsend_like(vh))
    vg[g] = vh[...].reshape(nh * ROWS, TILE)
    send_all(G_VEC, g_peer, ng, lambda p: vg.at[g], vg.at[g])

    wait(recv_sem.at[Y_CODE], ccode.at[pl.ds(0, ny - 1)])
    col_sel = jnp.concatenate(
        [
            onehot(widen(lambda s, p=p: ccode[p, s : s + 1, :]), y * (nz * ROWS))
            for p in range(ny)
        ],
        axis=0,
    )
    wait(recv_sem.at[Z_VEC], vz.at[pl.ds(0, nz - 1)])
    plane = vz[...].reshape(nz * ROWS, TILE)
    picked = jnp.dot(
        col_sel[:, : nz * ROWS].astype(jnp.bfloat16), plane, preferred_element_type=jnp.float32
    )
    ysend[...] = picked.astype(jnp.bfloat16).reshape(ny, SLOT_ROWS, TILE)
    send_all(Y_VEC, y_peer, ny, lambda p: ysend.at[p], yrecv.at[y])
    yrecv[y] = ysend[y]

    own_row_codes = widen(lambda s: row_codes[s : s + 1, :])
    slab_rows = ng * nh * ROWS
    pieces = [
        onehot(own_row_codes, b)[:, : min(LANES, slab_rows - b)]
        for b in range(0, slab_rows, LANES)
    ]
    row_sel = jnp.concatenate(pieces, axis=1).astype(jnp.bfloat16)
    half = lax.broadcasted_iota(jnp.int32, (8, TILE), 0) < 4

    def apply(vectors, contract):
        outs = []
        for k in range((slots + 1) // 2):
            pair = vectors[8 * k : 8 * k + 8].astype(jnp.bfloat16)
            both = [
                lax.dot_general(
                    pair,
                    tiles[min(2 * k + i, slots - 1)],
                    (((1,), (contract,)), ((), ())),
                    preferred_element_type=jnp.float32,
                )
                for i in range(2)
            ]
            outs.append(jnp.where(half, both[0], both[1]))
        return jnp.concatenate(outs, axis=0)[:live_rows]

    wait(recv_sem.at[G_VEC], vg.at[pl.ds(0, ng - 1)])
    row_vectors = jnp.dot(
        row_sel, vg[...].reshape(slab_rows, TILE), preferred_element_type=jnp.float32
    )
    locals_[4].wait()
    cprod[y, 0:live_rows, :] = apply(row_vectors, 0)
    mine = cprod.at[y, pl.ds(0, live_rows)]
    send_all(Y_PROD, y_peer, ny, lambda p: mine, mine)

    wait(recv_sem.at[Y_VEC], yrecv.at[pl.ds(0, ny - 1)])
    col_vectors = yrecv[0].astype(jnp.float32)
    for p in range(1, ny):
        col_vectors = col_vectors + yrecv[p].astype(jnp.float32)
    rprod[g, 0:live_rows, :] = apply(col_vectors, 1)
    mine_r = rprod.at[g, pl.ds(0, live_rows)]
    send_all(G_PROD, g_peer, ng, lambda p: mine_r, mine_r)

    col_place = col_sel.T[: nz * ROWS].astype(jnp.bfloat16)
    wait(recv_sem.at[G_CODE], rcode.at[pl.ds(0, ng - 1)])
    row_place = jnp.concatenate(
        [
            onehot(widen(lambda s, p=p: rcode[p, s : s + 1, :]), g * (nh * ROWS))
            for p in range(ng)
        ],
        axis=0,
    ).T[: nh * ROWS].astype(jnp.bfloat16)

    wait(recv_sem.at[Y_PROD], cprod.at[pl.ds(0, ny - 1), pl.ds(0, live_rows)])
    sums = place(col_place, cprod[...].reshape(ny * SLOT_ROWS, TILE))
    zsend[...] = sums.reshape(nz, ROWS, TILE)
    send_all(Z_PROD, z_peer, nz, lambda p: zsend.at[p], zrecv.at[z])
    zrecv[z] = zsend[z]

    wait(recv_sem.at[G_PROD], rprod.at[pl.ds(0, ng - 1), pl.ds(0, live_rows)])
    sums = place(row_place, rprod[...].reshape(ng * SLOT_ROWS, TILE))
    hsend[...] = sums.reshape(nh, ROWS, TILE)
    send(H_PROD, hsend.at[h_other], hrecv, h_id)
    total = hsend[h]

    wait(recv_sem.at[H_PROD], hrecv)
    total = total + hrecv[...]
    wait(recv_sem.at[Z_PROD], zrecv.at[pl.ds(0, nz - 1)])
    for p in range(nz):
        total = total + zrecv[p]
    for j in range(VB):
        out_ref[j] = total[NVEC * j : NVEC * (j + 1), :]

    wait(send_sem.at[H_VEC], hsend_like(vh))
    wait(send_sem.at[G_CODE], rcode.at[pl.ds(0, ng - 1)])
    wait(send_sem.at[Y_CODE], ccode.at[pl.ds(0, ny - 1)])
    wait(send_sem.at[Z_VEC], vz.at[pl.ds(0, nz - 1)])
    wait(send_sem.at[G_VEC], vg.at[pl.ds(0, ng - 1)])
    wait(send_sem.at[Y_VEC], ysend.at[pl.ds(0, ny - 1)])
    wait(send_sem.at[Y_PROD], cprod.at[pl.ds(0, ny - 1), pl.ds(0, live_rows)])
    wait(send_sem.at[G_PROD], rprod.at[pl.ds(0, ng - 1), pl.ds(0, live_rows)])
    wait(send_sem.at[Z_PROD], zsend.at[pl.ds(0, nz - 1)])
    wait(send_sem.at[H_PROD], hrecv)


def hsend_like(ref):
    return ref.at[0]


def on_device(sizes, vectors, tiles, tile_rows, tile_cols, tile_counts):
    ny, nz, nx, nh, nc = sizes
    ng = nx * nc
    slots = tiles.shape[2]
    bf16, f32, i32 = jnp.bfloat16, jnp.float32, jnp.int32
    vmem, smem = pltpu.VMEM, pltpu.SMEM
    return pl.pallas_call(
        functools.partial(kernel, sizes),
        out_shape=jax.ShapeDtypeStruct(vectors.shape, f32),
        in_specs=[pl.BlockSpec(memory_space=pltpu.HBM)] * 5,
        out_specs=pl.BlockSpec(memory_space=pltpu.VMEM),
        scratch_shapes=[
            vmem(vectors.shape, bf16),
            vmem(tiles.shape[2:], bf16),
            smem(tile_rows.shape, i32),
            smem(tile_cols.shape, i32),
            smem(tile_counts.shape, i32),
            vmem((nz, ROWS, TILE), bf16),
            vmem((nh, ROWS, TILE), bf16),
            vmem((ng, nh * ROWS, TILE), bf16),
            vmem((ny, PAD, LANES), i32),
            vmem((ng, PAD, LANES), i32),
            vmem((ny, SLOT_ROWS, TILE), bf16),
            vmem((ny, SLOT_ROWS, TILE), bf16),
            vmem((ny, SLOT_ROWS, TILE), f32),
            vmem((ng, SLOT_ROWS, TILE), f32),
            vmem((nz, ROWS, TILE), f32),
            vmem((nz, ROWS, TILE), f32),
            vmem((nh, ROWS, TILE), f32),
            vmem((ROWS, TILE), f32),
            pltpu.SemaphoreType.DMA((5,)),
            pltpu.SemaphoreType.DMA((10,)),
            pltpu.SemaphoreType.DMA((10,)),
        ],
        compiler_params=pltpu.CompilerParams(
            collective_id=0, has_side_effects=True, vmem_limit_bytes=60 * 2**20
        ),
        cost_estimate=pl.CostEstimate(
            flops=2**24, bytes_accessed=2**20, transcendentals=0
        ),
    )(vectors, tiles, tile_rows, tile_cols, tile_counts)


def build(mesh, nz, nh, nc):
    ny, nx = mesh.shape["row"] // nz, mesh.shape["col"] // (nh * nc)
    placed = (
        P(("row", "col"), None, None),
        P("row", "col", None, None, None),
        P("row", "col", None),
        P("row", "col", None),
        P("row", "col"),
    )
    return jax.shard_map(
        functools.partial(on_device, (ny, nz, nx, nh, nc)),
        mesh=mesh,
        in_specs=placed,
        out_specs=P(("row", "col"), None, None),
        check_vma=False,
    )


def solution(mesh):
    return build(mesh, 8, 2, 2)
```

```python
import functools

import jax
import jax.numpy as jnp
from jax import lax
from jax.experimental import pallas as pl
from jax.experimental.pallas import tpu as pltpu
from jax.sharding import PartitionSpec as P

MESH = pl.DeviceIdType.MESH
NVEC = 4
TILE = 256
VB = 4
ROWS = VB * NVEC
PAD = 8
SLOT_ROWS = PAD * NVEC
LANES = 128
NONE = -(2**20)

H_VEC, X_CODE, Y_CODE, Z_VEC, X_VEC, Y_VEC, Y_PROD, X_PROD, Z_PROD, H_PROD = range(10)


def widen(row_of):
    sub = lax.broadcasted_iota(jnp.int32, (8, LANES), 0)
    pieces = []
    for k in range(PAD // 2):
        low = jnp.broadcast_to(row_of(2 * k), (8, LANES))
        high = jnp.broadcast_to(row_of(2 * k + 1), (8, LANES))
        pieces.append(jnp.where(sub < 4, low, high) + (sub & 3))
    return jnp.concatenate(pieces, axis=0)


def onehot(codes, base):
    lane = lax.broadcasted_iota(jnp.int32, codes.shape, 1)
    return jnp.where(codes == lane + base, 1.0, 0.0).astype(jnp.float32)


def place(matrix, products):
    high = products.astype(jnp.bfloat16)
    low = (products - high.astype(jnp.float32)).astype(jnp.bfloat16)
    return jnp.dot(matrix, high, preferred_element_type=jnp.float32) + jnp.dot(
        matrix, low, preferred_element_type=jnp.float32
    )


def kernel(
    sizes,
    vec_hbm, tiles_hbm, rows_hbm, cols_hbm, counts_hbm,
    out_ref,
    vin, tiles, rows_s, cols_s, counts_s,
    vz, vw, vx, ccode, rcode, ysend, yrecv, cprod, rprod, zsend, zrecv, wsend, wrecv, col_place,
    local_sem, send_sem, recv_sem,
):
    ny, nz, nx, nh, nc = sizes
    nw = nh * nc
    slots = tiles.shape[0]
    live_rows = slots * NVEC
    row, col = lax.axis_index("row"), lax.axis_index("col")
    y, z = row // nz, row % nz
    x, w = col // nw, col % nw
    h = w // nc

    def at(y_, z_, x_, w_):
        return (y_ * nz + z_, x_ * nw + w_)

    def peers(me, n, place_of):
        out = []
        for k in sorted(range(1, n), key=lambda k: -min(k, n - k)):
            p = lax.rem(me + k, n)
            out.append((p, place_of(p)))
        return out

    y_peers = peers(y, ny, lambda p: at(p, z, x, w))
    z_peers = peers(z, nz, lambda p: at(y, p, x, w))
    x_peers = peers(x, nx, lambda p: at(y, z, p, w))
    w_peers = peers(w, nw, lambda p: at(y, z, x, p))

    locals_ = [
        pltpu.make_async_copy(src, dst, local_sem.at[i])
        for i, (src, dst) in enumerate(
            (
                (vec_hbm, vin),
                (rows_hbm, rows_s),
                (cols_hbm, cols_s),
                (counts_hbm, counts_s),
                (tiles_hbm.at[0, 0], tiles),
            )
        )
    ]
    locals_[0].start()
    barrier = pltpu.get_barrier_semaphore()
    everyone = [device_id for _, device_id in w_peers + z_peers + y_peers + x_peers]
    for device_id in everyone:
        pl.semaphore_signal(barrier, inc=1, device_id=device_id, device_id_type=MESH)
    for copy in locals_[1:]:
        copy.start()

    def send(which, src, dst, device_id):
        pltpu.make_async_remote_copy(
            src_ref=src,
            dst_ref=dst,
            send_sem=send_sem.at[which],
            recv_sem=recv_sem.at[which],
            device_id=device_id,
            device_id_type=MESH,
        ).start()

    def wait(sem, ref):
        pltpu.make_async_copy(ref, ref, sem).wait()

    def send_all(which, peers_, src_of, dst):
        for p, device_id in peers_:
            send(which, src_of(p), dst, device_id)

    tail = SLOT_ROWS - live_rows
    if tail:
        cprod[:, live_rows:, :] = jnp.zeros((ny, tail, TILE), jnp.float32)
        rprod[:, live_rows:, :] = jnp.zeros((nx, tail, TILE), jnp.float32)

    locals_[0].wait()
    own = jnp.concatenate([vin[j].astype(jnp.float32) for j in range(VB)], axis=0)
    own = own.astype(jnp.bfloat16)
    vz[z] = own
    vw[w] = own
    for i in (1, 2, 3):
        locals_[i].wait()
    live = counts_s[0, 0]
    sub = lax.broadcasted_iota(jnp.int32, (PAD, LANES), 0)
    col_codes = jnp.full((PAD, LANES), NONE, jnp.int32)
    row_codes = col_codes
    for s in range(slots):
        q = cols_s[0, 0, s] * NVEC
        p = rows_s[0, 0, s] * NVEC
        col_codes = jnp.where(sub == s, jnp.where(s < live, q, NONE), col_codes)
        row_codes = jnp.where(sub == s, jnp.where(s < live, p, NONE), row_codes)
    ccode[y] = col_codes
    rcode[x] = row_codes

    own_row_codes = widen(lambda s: row_codes[s : s + 1, :])
    slab_rows = nx * nw * ROWS
    pieces = [
        onehot(own_row_codes, b)[:, : min(LANES, slab_rows - b)]
        for b in range(0, slab_rows, LANES)
    ]
    row_sel = jnp.concatenate(pieces, axis=1).astype(jnp.bfloat16)
    half = lax.broadcasted_iota(jnp.int32, (8, TILE), 0) < 4

    def apply(vectors, contract):
        outs = []
        for k in range((slots + 1) // 2):
            pair = vectors[8 * k : 8 * k + 8].astype(jnp.bfloat16)
            both = [
                lax.dot_general(
                    pair,
                    tiles[min(2 * k + i, slots - 1)],
                    (((1,), (contract,)), ((), ())),
                    preferred_element_type=jnp.float32,
                )
                for i in range(2)
            ]
            outs.append(jnp.where(half, both[0], both[1]))
        return jnp.concatenate(outs, axis=0)[:live_rows]

    pl.semaphore_wait(barrier, len(everyone))

    send_all(H_VEC, w_peers, lambda p: vw.at[w], vw.at[w])
    send_all(Z_VEC, z_peers, lambda p: vz.at[z], vz.at[z])
    send_all(Y_CODE, y_peers, lambda p: ccode.at[y], ccode.at[y])
    send_all(X_CODE, x_peers, lambda p: rcode.at[x], rcode.at[x])

    def slab_vectors():
        wait(recv_sem.at[H_VEC], vw.at[pl.ds(0, nw - 1)])
        vx[x] = vw[...].reshape(nw * ROWS, TILE)
        send_all(X_VEC, x_peers, lambda p: vx.at[x], vx.at[x])

    def column_products():
        wait(recv_sem.at[X_VEC], vx.at[pl.ds(0, nx - 1)])
        row_vectors = jnp.dot(
            row_sel, vx[...].reshape(slab_rows, TILE), preferred_element_type=jnp.float32
        )
        cprod[y, 0:live_rows, :] = apply(row_vectors, 0)
        mine = cprod.at[y, pl.ds(0, live_rows)]
        send_all(Y_PROD, y_peers, lambda p: mine, mine)

    def column_sums():
        wait(recv_sem.at[Y_PROD], cprod.at[pl.ds(0, ny - 1), pl.ds(0, live_rows)])
        sums = place(col_place[...], cprod[...].reshape(ny * SLOT_ROWS, TILE))
        zsend[...] = sums.reshape(nz, ROWS, TILE)
        send_all(Z_PROD, z_peers, lambda p: zsend.at[p], zrecv.at[z])
        zrecv[z] = zsend[z]

    columns_first = h == 0

    pl.when(columns_first)(slab_vectors)

    wait(recv_sem.at[Y_CODE], ccode.at[pl.ds(0, ny - 1)])
    col_sel = jnp.concatenate(
        [
            onehot(widen(lambda s, p=p: ccode[p, s : s + 1, :]), y * (nz * ROWS))
            for p in range(ny)
        ],
        axis=0,
    )
    wait(recv_sem.at[Z_VEC], vz.at[pl.ds(0, nz - 1)])
    plane = vz[...].reshape(nz * ROWS, TILE)
    picked = jnp.dot(
        col_sel[:, : nz * ROWS].astype(jnp.bfloat16), plane, preferred_element_type=jnp.float32
    )
    ysend[...] = picked.astype(jnp.bfloat16).reshape(ny, SLOT_ROWS, TILE)
    send_all(Y_VEC, y_peers, lambda p: ysend.at[p], yrecv.at[y])
    yrecv[y] = ysend[y]

    pl.when(jnp.logical_not(columns_first))(slab_vectors)

    wait(recv_sem.at[X_CODE], rcode.at[pl.ds(0, nx - 1)])
    row_place = jnp.concatenate(
        [
            onehot(widen(lambda s, p=p: rcode[p, s : s + 1, :]), x * (nw * ROWS))
            for p in range(nx)
        ],
        axis=0,
    ).T[: nw * ROWS].astype(jnp.bfloat16)
    col_place[...] = col_sel.T[: nz * ROWS].astype(jnp.bfloat16)
    locals_[4].wait()

    pl.when(columns_first)(column_products)

    wait(recv_sem.at[Y_VEC], yrecv.at[pl.ds(0, ny - 1)])
    col_vectors = yrecv[0].astype(jnp.float32)
    for p in range(1, ny):
        col_vectors = col_vectors + yrecv[p].astype(jnp.float32)
    rprod[x, 0:live_rows, :] = apply(col_vectors, 1)
    mine_r = rprod.at[x, pl.ds(0, live_rows)]
    send_all(X_PROD, x_peers, lambda p: mine_r, mine_r)

    pl.when(jnp.logical_not(columns_first))(column_products)

    pl.when(columns_first)(column_sums)

    wait(recv_sem.at[X_PROD], rprod.at[pl.ds(0, nx - 1), pl.ds(0, live_rows)])
    sums = place(row_place, rprod[...].reshape(nx * SLOT_ROWS, TILE))
    wsend[...] = sums.reshape(nw, ROWS, TILE)
    send_all(H_PROD, w_peers, lambda p: wsend.at[p], wrecv.at[w])
    wrecv[w] = wsend[w]

    pl.when(jnp.logical_not(columns_first))(column_sums)

    wait(recv_sem.at[H_PROD], wrecv.at[pl.ds(0, nw - 1)])
    total = wrecv[0]
    for p in range(1, nw):
        total = total + wrecv[p]
    wait(recv_sem.at[Z_PROD], zrecv.at[pl.ds(0, nz - 1)])
    for p in range(nz):
        total = total + zrecv[p]
    for j in range(VB):
        out_ref[j] = total[NVEC * j : NVEC * (j + 1), :]

    wait(send_sem.at[H_VEC], vw.at[pl.ds(0, nw - 1)])
    wait(send_sem.at[X_CODE], rcode.at[pl.ds(0, nx - 1)])
    wait(send_sem.at[Y_CODE], ccode.at[pl.ds(0, ny - 1)])
    wait(send_sem.at[Z_VEC], vz.at[pl.ds(0, nz - 1)])
    wait(send_sem.at[X_VEC], vx.at[pl.ds(0, nx - 1)])
    wait(send_sem.at[Y_VEC], ysend.at[pl.ds(0, ny - 1)])
    wait(send_sem.at[Y_PROD], cprod.at[pl.ds(0, ny - 1), pl.ds(0, live_rows)])
    wait(send_sem.at[X_PROD], rprod.at[pl.ds(0, nx - 1), pl.ds(0, live_rows)])
    wait(send_sem.at[Z_PROD], zsend.at[pl.ds(0, nz - 1)])
    wait(send_sem.at[H_PROD], wsend.at[pl.ds(0, nw - 1)])


def on_device(sizes, vectors, tiles, tile_rows, tile_cols, tile_counts):
    ny, nz, nx, nh, nc = sizes
    nw = nh * nc
    bf16, f32, i32 = jnp.bfloat16, jnp.float32, jnp.int32
    vmem, smem = pltpu.VMEM, pltpu.SMEM
    return pl.pallas_call(
        functools.partial(kernel, sizes),
        out_shape=jax.ShapeDtypeStruct(vectors.shape, f32),
        in_specs=[pl.BlockSpec(memory_space=pltpu.HBM)] * 5,
        out_specs=pl.BlockSpec(memory_space=pltpu.VMEM),
        scratch_shapes=[
            vmem(vectors.shape, bf16),
            vmem(tiles.shape[2:], bf16),
            smem(tile_rows.shape, i32),
            smem(tile_cols.shape, i32),
            smem(tile_counts.shape, i32),
            vmem((nz, ROWS, TILE), bf16),
            vmem((nw, ROWS, TILE), bf16),
            vmem((nx, nw * ROWS, TILE), bf16),
            vmem((ny, PAD, LANES), i32),
            vmem((nx, PAD, LANES), i32),
            vmem((ny, SLOT_ROWS, TILE), bf16),
            vmem((ny, SLOT_ROWS, TILE), bf16),
            vmem((ny, SLOT_ROWS, TILE), f32),
            vmem((nx, SLOT_ROWS, TILE), f32),
            vmem((nz, ROWS, TILE), f32),
            vmem((nz, ROWS, TILE), f32),
            vmem((nw, ROWS, TILE), f32),
            vmem((nw, ROWS, TILE), f32),
            vmem((nz * ROWS, ny * SLOT_ROWS), bf16),
            pltpu.SemaphoreType.DMA((5,)),
            pltpu.SemaphoreType.DMA((10,)),
            pltpu.SemaphoreType.DMA((10,)),
        ],
        compiler_params=pltpu.CompilerParams(
            collective_id=0, has_side_effects=True, vmem_limit_bytes=55000 * 2**10
        ),
        cost_estimate=pl.CostEstimate(
            flops=2**24, bytes_accessed=2**20, transcendentals=0
        ),
    )(vectors, tiles, tile_rows, tile_cols, tile_counts)


def build(mesh, nz, nh, nc):
    ny, nx = mesh.shape["row"] // nz, mesh.shape["col"] // (nh * nc)
    placed = (
        P(("row", "col"), None, None),
        P("row", "col", None, None, None),
        P("row", "col", None),
        P("row", "col", None),
        P("row", "col"),
    )
    return jax.shard_map(
        functools.partial(on_device, (ny, nz, nx, nh, nc)),
        mesh=mesh,
        in_specs=placed,
        out_specs=P(("row", "col"), None, None),
        check_vma=False,
    )


def solution(mesh):
    return build(mesh, 8, 2, 2)
```

```python
import functools

import jax
import jax.numpy as jnp
from jax import lax
from jax.experimental import pallas as pl
from jax.experimental.pallas import tpu as pltpu
from jax.sharding import PartitionSpec as P

MESH = pl.DeviceIdType.MESH
NVEC = 4
TILE = 256
VB = 4
ROWS = VB * NVEC
PAD = 8
SLOT_ROWS = PAD * NVEC
LANES = 128
NONE = -(2**20)

GROUPS = 13
H_VEC, X_CODE, Y_CODE, Z_CODE, Z_VEC, X_VEC, Y_VEC = range(7)
Y_PROD, Z_SUM, Z_PROD, Y_SUM, X_PROD, H_PROD = range(7, GROUPS)


def widen(row_of):
    sub = lax.broadcasted_iota(jnp.int32, (8, LANES), 0)
    pieces = []
    for k in range(PAD // 2):
        low = jnp.broadcast_to(row_of(2 * k), (8, LANES))
        high = jnp.broadcast_to(row_of(2 * k + 1), (8, LANES))
        pieces.append(jnp.where(sub < 4, low, high) + (sub & 3))
    return jnp.concatenate(pieces, axis=0)


def onehot(codes, base, gap=0):
    lane = lax.broadcasted_iota(jnp.int32, codes.shape, 1)
    target = lane + base + (lane // ROWS) * gap
    return jnp.where(codes == target, 1.0, 0.0).astype(jnp.float32)


def place(matrix, products):
    high = products.astype(jnp.bfloat16)
    low = (products - high.astype(jnp.float32)).astype(jnp.bfloat16)
    return jnp.dot(matrix, high, preferred_element_type=jnp.float32) + jnp.dot(
        matrix, low, preferred_element_type=jnp.float32
    )


def kernel(
    sizes,
    vec_hbm, tiles_hbm, rows_hbm, cols_hbm, counts_hbm,
    out_ref,
    vin, tiles, rows_s, cols_s, counts_s,
    vz, vw, vx, ccode, zcode, rcode, ysend, yrecv, yprod, zprod, rprod,
    zsend, zrecv, ssend, srecv, wsend, wrecv, y_place, z_place,
    local_sem, send_sem, recv_sem,
):
    ny, nz, nx, nh, nc = sizes
    nw = nh * nc
    slots = tiles.shape[0]
    live_rows = slots * NVEC
    row, col = lax.axis_index("row"), lax.axis_index("col")
    y, z = row // nz, row % nz
    x, w = col // nw, col % nw
    h = w // nc

    def at(y_, z_, x_, w_):
        return (y_ * nz + z_, x_ * nw + w_)

    def peers(me, n, place_of):
        out = []
        for k in sorted(range(1, n), key=lambda k: -min(k, n - k)):
            p = lax.rem(me + k, n)
            out.append((p, place_of(p)))
        return out

    y_peers = peers(y, ny, lambda p: at(p, z, x, w))
    z_peers = peers(z, nz, lambda p: at(y, p, x, w))
    x_peers = peers(x, nx, lambda p: at(y, z, p, w))
    w_peers = peers(w, nw, lambda p: at(y, z, x, p))

    locals_ = [
        pltpu.make_async_copy(src, dst, local_sem.at[i])
        for i, (src, dst) in enumerate(
            (
                (vec_hbm, vin),
                (rows_hbm, rows_s),
                (cols_hbm, cols_s),
                (counts_hbm, counts_s),
                (tiles_hbm.at[0, 0], tiles),
            )
        )
    ]
    locals_[0].start()
    barrier = pltpu.get_barrier_semaphore()
    everyone = [device_id for _, device_id in w_peers + z_peers + y_peers + x_peers]
    for device_id in everyone:
        pl.semaphore_signal(barrier, inc=1, device_id=device_id, device_id_type=MESH)
    for copy in locals_[1:]:
        copy.start()

    def send(which, src, dst, device_id):
        pltpu.make_async_remote_copy(
            src_ref=src,
            dst_ref=dst,
            send_sem=send_sem.at[which],
            recv_sem=recv_sem.at[which],
            device_id=device_id,
            device_id_type=MESH,
        ).start()

    def wait(sem, ref):
        pltpu.make_async_copy(ref, ref, sem).wait()

    def send_all(which, peers_, src_of, dst):
        for p, device_id in peers_:
            send(which, src_of(p), dst, device_id)

    tail = SLOT_ROWS - live_rows
    if tail:
        yprod[:, live_rows:, :] = jnp.zeros((ny, tail, LANES), jnp.float32)
        zprod[:, live_rows:, :] = jnp.zeros((nz, tail, LANES), jnp.float32)
        rprod[:, live_rows:, :] = jnp.zeros((nx, tail, TILE), jnp.float32)

    locals_[0].wait()
    own = jnp.concatenate([vin[j].astype(jnp.float32) for j in range(VB)], axis=0)
    own = own.astype(jnp.bfloat16)
    vz[z] = own
    vw[w] = own
    for i in (1, 2, 3):
        locals_[i].wait()
    live = counts_s[0, 0]
    sub = lax.broadcasted_iota(jnp.int32, (PAD, LANES), 0)
    col_codes = jnp.full((PAD, LANES), NONE, jnp.int32)
    row_codes = col_codes
    for s in range(slots):
        q = cols_s[0, 0, s] * NVEC
        p = rows_s[0, 0, s] * NVEC
        col_codes = jnp.where(sub == s, jnp.where(s < live, q, NONE), col_codes)
        row_codes = jnp.where(sub == s, jnp.where(s < live, p, NONE), row_codes)
    ccode[y] = col_codes
    zcode[z] = col_codes
    rcode[x] = row_codes

    own_row_codes = widen(lambda s: row_codes[s : s + 1, :])
    slab_rows = nx * nw * ROWS
    pieces = [
        onehot(own_row_codes, b)[:, : min(LANES, slab_rows - b)]
        for b in range(0, slab_rows, LANES)
    ]
    row_sel = jnp.concatenate(pieces, axis=1).astype(jnp.bfloat16)
    half = lax.broadcasted_iota(jnp.int32, (8, TILE), 0) < 4

    def apply(vectors, contract):
        outs = []
        for k in range((slots + 1) // 2):
            pair = vectors[8 * k : 8 * k + 8].astype(jnp.bfloat16)
            both = [
                lax.dot_general(
                    pair,
                    tiles[min(2 * k + i, slots - 1)],
                    (((1,), (contract,)), ((), ())),
                    preferred_element_type=jnp.float32,
                )
                for i in range(2)
            ]
            outs.append(jnp.where(half, both[0], both[1]))
        return jnp.concatenate(outs, axis=0)[:live_rows]

    pl.semaphore_wait(barrier, len(everyone))

    send_all(H_VEC, w_peers, lambda p: vw.at[w], vw.at[w])
    send_all(Z_VEC, z_peers, lambda p: vz.at[z], vz.at[z])
    send_all(Y_CODE, y_peers, lambda p: ccode.at[y], ccode.at[y])
    send_all(X_CODE, x_peers, lambda p: rcode.at[x], rcode.at[x])

    def slab_vectors():
        wait(recv_sem.at[H_VEC], vw.at[pl.ds(0, nw - 1)])
        vx[x] = vw[...].reshape(nw * ROWS, TILE)
        send_all(X_VEC, x_peers, lambda p: vx.at[x], vx.at[x])

    def column_products():
        wait(recv_sem.at[X_VEC], vx.at[pl.ds(0, nx - 1)])
        row_vectors = jnp.dot(
            row_sel, vx[...].reshape(slab_rows, TILE), preferred_element_type=jnp.float32
        )
        products = apply(row_vectors, 0)
        zprod[z, 0:live_rows, :] = products[:, LANES:]
        mine_z = zprod.at[z, pl.ds(0, live_rows)]
        send_all(Z_PROD, z_peers, lambda p: mine_z, mine_z)
        yprod[y, 0:live_rows, :] = products[:, :LANES]
        mine_y = yprod.at[y, pl.ds(0, live_rows)]
        send_all(Y_PROD, y_peers, lambda p: mine_y, mine_y)

    def column_sums():
        wait(recv_sem.at[Y_PROD], yprod.at[pl.ds(0, ny - 1), pl.ds(0, live_rows)])
        sums = place(y_place[...], yprod[...].reshape(ny * SLOT_ROWS, LANES))
        zsend[...] = sums.reshape(nz, ROWS, LANES)
        send_all(Z_SUM, z_peers, lambda p: zsend.at[p], zrecv.at[z])
        zrecv[z] = zsend[z]
        wait(recv_sem.at[Z_PROD], zprod.at[pl.ds(0, nz - 1), pl.ds(0, live_rows)])
        sums = place(z_place[...], zprod[...].reshape(nz * SLOT_ROWS, LANES))
        ssend[...] = sums.reshape(ny, ROWS, LANES)
        send_all(Y_SUM, y_peers, lambda p: ssend.at[p], srecv.at[y])
        srecv[y] = ssend[y]

    columns_first = h == 0

    pl.when(columns_first)(slab_vectors)

    wait(recv_sem.at[Y_CODE], ccode.at[pl.ds(0, ny - 1)])
    col_sel = jnp.concatenate(
        [
            onehot(widen(lambda s, p=p: ccode[p, s : s + 1, :]), y * (nz * ROWS))
            for p in range(ny)
        ],
        axis=0,
    )
    wait(recv_sem.at[Z_VEC], vz.at[pl.ds(0, nz - 1)])
    plane = vz[...].reshape(nz * ROWS, TILE)
    picked = jnp.dot(
        col_sel[:, : nz * ROWS].astype(jnp.bfloat16), plane, preferred_element_type=jnp.float32
    )
    for p in range(ny):
        some = picked[SLOT_ROWS * p : SLOT_ROWS * p + live_rows]
        both = jnp.concatenate([some[:, :LANES], some[:, LANES:]], axis=0)
        ysend[p] = both.astype(jnp.bfloat16)
    send_all(Y_VEC, y_peers, lambda p: ysend.at[p], yrecv.at[y])
    yrecv[y] = ysend[y]
    send_all(Z_CODE, z_peers, lambda p: zcode.at[z], zcode.at[z])

    pl.when(jnp.logical_not(columns_first))(slab_vectors)

    wait(recv_sem.at[X_CODE], rcode.at[pl.ds(0, nx - 1)])
    row_place = jnp.concatenate(
        [
            onehot(widen(lambda s, p=p: rcode[p, s : s + 1, :]), x * (nw * ROWS))
            for p in range(nx)
        ],
        axis=0,
    ).T[: nw * ROWS].astype(jnp.bfloat16)
    y_place[...] = col_sel.T[: nz * ROWS].astype(jnp.bfloat16)
    locals_[4].wait()

    pl.when(columns_first)(column_products)

    wait(recv_sem.at[Y_VEC], yrecv.at[pl.ds(0, ny - 1)])
    col_vectors = yrecv[0].astype(jnp.float32)
    for p in range(1, ny):
        col_vectors = col_vectors + yrecv[p].astype(jnp.float32)
    col_vectors = jnp.concatenate([col_vectors[:live_rows], col_vectors[live_rows:]], axis=1)
    rprod[x, 0:live_rows, :] = apply(col_vectors, 1)
    mine_r = rprod.at[x, pl.ds(0, live_rows)]
    send_all(X_PROD, x_peers, lambda p: mine_r, mine_r)

    pl.when(jnp.logical_not(columns_first))(column_products)

    wait(recv_sem.at[Z_CODE], zcode.at[pl.ds(0, nz - 1)])
    z_place[...] = jnp.concatenate(
        [
            onehot(widen(lambda s, p=p: zcode[p, s : s + 1, :]), z * ROWS, (nz - 1) * ROWS)
            for p in range(nz)
        ],
        axis=0,
    ).T[: ny * ROWS].astype(jnp.bfloat16)

    pl.when(columns_first)(column_sums)

    wait(recv_sem.at[X_PROD], rprod.at[pl.ds(0, nx - 1), pl.ds(0, live_rows)])
    sums = place(row_place, rprod[...].reshape(nx * SLOT_ROWS, TILE))
    wsend[...] = sums.reshape(nw, ROWS, TILE)
    send_all(H_PROD, w_peers, lambda p: wsend.at[p], wrecv.at[w])
    wrecv[w] = wsend[w]

    pl.when(jnp.logical_not(columns_first))(column_sums)

    wait(recv_sem.at[H_PROD], wrecv.at[pl.ds(0, nw - 1)])
    total = wrecv[0]
    for p in range(1, nw):
        total = total + wrecv[p]
    wait(recv_sem.at[Y_SUM], srecv.at[pl.ds(0, ny - 1)])
    right = srecv[0]
    for p in range(1, ny):
        right = right + srecv[p]
    wait(recv_sem.at[Z_SUM], zrecv.at[pl.ds(0, nz - 1)])
    left = zrecv[0]
    for p in range(1, nz):
        left = left + zrecv[p]
    total = total + jnp.concatenate([left, right], axis=1)
    for j in range(VB):
        out_ref[j] = total[NVEC * j : NVEC * (j + 1), :]

    wait(send_sem.at[H_VEC], vw.at[pl.ds(0, nw - 1)])
    wait(send_sem.at[X_CODE], rcode.at[pl.ds(0, nx - 1)])
    wait(send_sem.at[Y_CODE], ccode.at[pl.ds(0, ny - 1)])
    wait(send_sem.at[Z_VEC], vz.at[pl.ds(0, nz - 1)])
    wait(send_sem.at[X_VEC], vx.at[pl.ds(0, nx - 1)])
    wait(send_sem.at[Y_VEC], ysend.at[pl.ds(0, ny - 1)])
    wait(send_sem.at[Z_CODE], zcode.at[pl.ds(0, nz - 1)])
    wait(send_sem.at[Y_PROD], yprod.at[pl.ds(0, ny - 1), pl.ds(0, live_rows)])
    wait(send_sem.at[Z_PROD], zprod.at[pl.ds(0, nz - 1), pl.ds(0, live_rows)])
    wait(send_sem.at[X_PROD], rprod.at[pl.ds(0, nx - 1), pl.ds(0, live_rows)])
    wait(send_sem.at[Z_SUM], zsend.at[pl.ds(0, nz - 1)])
    wait(send_sem.at[Y_SUM], ssend.at[pl.ds(0, ny - 1)])
    wait(send_sem.at[H_PROD], wsend.at[pl.ds(0, nw - 1)])


def on_device(sizes, vectors, tiles, tile_rows, tile_cols, tile_counts):
    ny, nz, nx, nh, nc = sizes
    nw = nh * nc
    live_rows = tiles.shape[2] * NVEC
    bf16, f32, i32 = jnp.bfloat16, jnp.float32, jnp.int32
    vmem, smem = pltpu.VMEM, pltpu.SMEM
    return pl.pallas_call(
        functools.partial(kernel, sizes),
        out_shape=jax.ShapeDtypeStruct(vectors.shape, f32),
        in_specs=[pl.BlockSpec(memory_space=pltpu.HBM)] * 5,
        out_specs=pl.BlockSpec(memory_space=pltpu.VMEM),
        scratch_shapes=[
            vmem(vectors.shape, bf16),
            vmem(tiles.shape[2:], bf16),
            smem(tile_rows.shape, i32),
            smem(tile_cols.shape, i32),
            smem(tile_counts.shape, i32),
            vmem((nz, ROWS, TILE), bf16),
            vmem((nw, ROWS, TILE), bf16),
            vmem((nx, nw * ROWS, TILE), bf16),
            vmem((ny, PAD, LANES), i32),
            vmem((nz, PAD, LANES), i32),
            vmem((nx, PAD, LANES), i32),
            vmem((ny, 2 * live_rows, LANES), bf16),
            vmem((ny, 2 * live_rows, LANES), bf16),
            vmem((ny, SLOT_ROWS, LANES), f32),
            vmem((nz, SLOT_ROWS, LANES), f32),
            vmem((nx, SLOT_ROWS, TILE), f32),
            vmem((nz, ROWS, LANES), f32),
            vmem((nz, ROWS, LANES), f32),
            vmem((ny, ROWS, LANES), f32),
            vmem((ny, ROWS, LANES), f32),
            vmem((nw, ROWS, TILE), f32),
            vmem((nw, ROWS, TILE), f32),
            vmem((nz * ROWS, ny * SLOT_ROWS), bf16),
            vmem((ny * ROWS, nz * SLOT_ROWS), bf16),
            pltpu.SemaphoreType.DMA((5,)),
            pltpu.SemaphoreType.DMA((GROUPS,)),
            pltpu.SemaphoreType.DMA((GROUPS,)),
        ],
        compiler_params=pltpu.CompilerParams(
            collective_id=0, has_side_effects=True, vmem_limit_bytes=55000 * 2**10
        ),
        cost_estimate=pl.CostEstimate(
            flops=2**24, bytes_accessed=2**20, transcendentals=0
        ),
    )(vectors, tiles, tile_rows, tile_cols, tile_counts)


def build(mesh, nz, nh, nc):
    ny, nx = mesh.shape["row"] // nz, mesh.shape["col"] // (nh * nc)
    placed = (
        P(("row", "col"), None, None),
        P("row", "col", None, None, None),
        P("row", "col", None),
        P("row", "col", None),
        P("row", "col"),
    )
    return jax.shard_map(
        functools.partial(on_device, (ny, nz, nx, nh, nc)),
        mesh=mesh,
        in_specs=placed,
        out_specs=P(("row", "col"), None, None),
        check_vma=False,
    )


def solution(mesh):
    return build(mesh, 8, 2, 2)
```

```python
import functools

import jax
import jax.numpy as jnp
from jax import lax
from jax.experimental import pallas as pl
from jax.experimental.pallas import tpu as pltpu
from jax.sharding import PartitionSpec as P

MESH = pl.DeviceIdType.MESH
NVEC = 4
TILE = 256
VB = 4
ROWS = VB * NVEC
PAD = 8
SLOT_ROWS = PAD * NVEC
LANES = 128
NONE = -(2**20)

GROUPS = 15
C_VEC, H_VEC, X_CODE, Y_CODE, Z_CODE, Z_VEC, X_NEAR, X_FAR, Y_VEC = range(9)
Y_PROD, Z_SUM, Z_PROD, Y_SUM, X_PROD, H_PROD = range(9, GROUPS)


def widen(row_of):
    sub = lax.broadcasted_iota(jnp.int32, (8, LANES), 0)
    pieces = []
    for k in range(PAD // 2):
        low = jnp.broadcast_to(row_of(2 * k), (8, LANES))
        high = jnp.broadcast_to(row_of(2 * k + 1), (8, LANES))
        pieces.append(jnp.where(sub < 4, low, high) + (sub & 3))
    return jnp.concatenate(pieces, axis=0)


def onehot(codes, base, gap=0):
    lane = lax.broadcasted_iota(jnp.int32, codes.shape, 1)
    target = lane + base + (lane // ROWS) * gap
    return jnp.where(codes == target, 1.0, 0.0).astype(jnp.float32)


def place(matrix, products):
    high = products.astype(jnp.bfloat16)
    low = (products - high.astype(jnp.float32)).astype(jnp.bfloat16)
    return jnp.dot(matrix, high, preferred_element_type=jnp.float32) + jnp.dot(
        matrix, low, preferred_element_type=jnp.float32
    )


def kernel(
    sizes,
    vec_hbm, tiles_hbm, rows_hbm, cols_hbm, counts_hbm,
    out_ref,
    vin, tiles, rows_s, cols_s, counts_s,
    vz, vx, ccode, zcode, rcode, ysend, yrecv, yprod, zprod, rprod,
    zsend, zrecv, ssend, srecv, wsend, wrecv, y_place, z_place,
    local_sem, send_sem, recv_sem,
):
    ny, nz, nx, nh, nc = sizes
    nw = nh * nc
    slots = tiles.shape[0]
    live_rows = slots * NVEC
    row, col = lax.axis_index("row"), lax.axis_index("col")
    y, z = row // nz, row % nz
    x, w = col // nw, col % nw
    h = w // nc

    def at(y_, z_, x_, w_):
        return (y_ * nz + z_, x_ * nw + w_)

    def peers(me, n, place_of, line=False):
        out = []
        for k in sorted(range(1, n), key=lambda k: min(k, n - k) * (1 if line else -1)):
            p = lax.rem(me + k, n)
            out.append((p, place_of(p)))
        return out

    y_peers = peers(y, ny, lambda p: at(p, z, x, w))
    z_peers = peers(z, nz, lambda p: at(y, p, x, w), line=True)
    x_peers = peers(x, nx, lambda p: at(y, z, p, w))
    cores = [h * nc + lax.rem(w + k, nc) for k in range(nc)]
    core_peers = [(p, at(y, z, x, p)) for p in cores[1:]]
    far_peers = [(p, at(y, z, x, p)) for p in [nw - nc - h * nc + (c - h * nc) for c in cores]]
    w_peers = far_peers + core_peers

    locals_ = [
        pltpu.make_async_copy(src, dst, local_sem.at[i])
        for i, (src, dst) in enumerate(
            (
                (vec_hbm, vin),
                (rows_hbm, rows_s),
                (cols_hbm, cols_s),
                (counts_hbm, counts_s),
                (tiles_hbm.at[0, 0], tiles),
            )
        )
    ]
    locals_[0].start()
    barrier = pltpu.get_barrier_semaphore()
    ordered = w_peers[:1] + y_peers[:3] + z_peers[:5] + w_peers[1:] + y_peers[3:] + x_peers + z_peers[5:]
    everyone = [device_id for _, device_id in ordered]
    for device_id in everyone:
        pl.semaphore_signal(barrier, inc=1, device_id=device_id, device_id_type=MESH)
    for copy in locals_[1:]:
        copy.start()

    def send(which, src, dst, device_id):
        pltpu.make_async_remote_copy(
            src_ref=src,
            dst_ref=dst,
            send_sem=send_sem.at[which],
            recv_sem=recv_sem.at[which],
            device_id=device_id,
            device_id_type=MESH,
        ).start()

    def wait(sem, ref):
        pltpu.make_async_copy(ref, ref, sem).wait()

    def send_all(which, peers_, src_of, dst):
        for p, device_id in peers_:
            send(which, src_of(p), dst, device_id)

    tail = SLOT_ROWS - live_rows
    if tail:
        yprod[:, live_rows:, :] = jnp.zeros((ny, tail, LANES), jnp.float32)
        zprod[:, live_rows:, :] = jnp.zeros((nz, tail, LANES), jnp.float32)
        rprod[:, live_rows:, :] = jnp.zeros((nx, tail, TILE), jnp.float32)

    locals_[0].wait()
    own = jnp.concatenate([vin[j].astype(jnp.float32) for j in range(VB)], axis=0)
    own = own.astype(jnp.bfloat16)
    vz[z] = own
    vx[x, w] = own
    for i in (1, 2, 3):
        locals_[i].wait()
    live = counts_s[0, 0]
    sub = lax.broadcasted_iota(jnp.int32, (PAD, LANES), 0)
    col_codes = jnp.full((PAD, LANES), NONE, jnp.int32)
    row_codes = col_codes
    for s in range(slots):
        q = cols_s[0, 0, s] * NVEC
        p = rows_s[0, 0, s] * NVEC
        col_codes = jnp.where(sub == s, jnp.where(s < live, q, NONE), col_codes)
        row_codes = jnp.where(sub == s, jnp.where(s < live, p, NONE), row_codes)
    ccode[y] = col_codes
    zcode[z] = col_codes
    rcode[x] = row_codes

    own_row_codes = widen(lambda s: row_codes[s : s + 1, :])
    slab_rows = nx * nw * ROWS
    pieces = [
        onehot(own_row_codes, b)[:, : min(LANES, slab_rows - b)]
        for b in range(0, slab_rows, LANES)
    ]
    row_sel = jnp.concatenate(pieces, axis=1).astype(jnp.bfloat16)
    half = lax.broadcasted_iota(jnp.int32, (8, TILE), 0) < 4

    def apply(vectors, contract):
        outs = []
        for k in range((slots + 1) // 2):
            pair = vectors[8 * k : 8 * k + 8].astype(jnp.bfloat16)
            both = [
                lax.dot_general(
                    pair,
                    tiles[min(2 * k + i, slots - 1)],
                    (((1,), (contract,)), ((), ())),
                    preferred_element_type=jnp.float32,
                )
                for i in range(2)
            ]
            outs.append(jnp.where(half, both[0], both[1]))
        return jnp.concatenate(outs, axis=0)[:live_rows]

    pl.semaphore_wait(barrier, len(everyone))

    send_all(H_VEC, far_peers, lambda p: vx.at[x, w], vx.at[x, w])
    send_all(C_VEC, core_peers, lambda p: vx.at[x, w], vx.at[x, w])
    send_all(Z_VEC, z_peers, lambda p: vz.at[z], vz.at[z])
    send_all(Y_CODE, y_peers, lambda p: ccode.at[y], ccode.at[y])
    send_all(X_CODE, x_peers, lambda p: rcode.at[x], rcode.at[x])

    def slab_vectors():
        wait(recv_sem.at[C_VEC], vx.at[0, pl.ds(0, nc - 1)])
        near = vx.at[x, pl.ds(h * nc, nc)]
        send_all(X_NEAR, x_peers, lambda p: near, near)
        wait(recv_sem.at[H_VEC], vx.at[0, pl.ds(0, nw - nc)])
        far = vx.at[x, pl.ds((nh - 1 - h) * nc, nc)]
        send_all(X_FAR, x_peers, lambda p: far, far)

    def column_products():
        wait(recv_sem.at[X_NEAR], vx.at[pl.ds(0, nx - 1), pl.ds(0, nc)])
        wait(recv_sem.at[X_FAR], vx.at[pl.ds(0, nx - 1), pl.ds(0, nw - nc)])
        row_vectors = jnp.dot(
            row_sel, vx[...].reshape(slab_rows, TILE), preferred_element_type=jnp.float32
        )
        products = apply(row_vectors, 0)
        zprod[z, 0:live_rows, :] = products[:, LANES:]
        mine_z = zprod.at[z, pl.ds(0, live_rows)]
        send_all(Z_PROD, z_peers, lambda p: mine_z, mine_z)
        yprod[y, 0:live_rows, :] = products[:, :LANES]
        mine_y = yprod.at[y, pl.ds(0, live_rows)]
        send_all(Y_PROD, y_peers, lambda p: mine_y, mine_y)

    def column_sums():
        wait(recv_sem.at[Y_PROD], yprod.at[pl.ds(0, ny - 1), pl.ds(0, live_rows)])
        sums = place(y_place[...], yprod[...].reshape(ny * SLOT_ROWS, LANES))
        zsend[...] = sums.reshape(nz, ROWS, LANES)
        send_all(Z_SUM, z_peers, lambda p: zsend.at[p], zrecv.at[z])
        zrecv[z] = zsend[z]
        wait(recv_sem.at[Z_PROD], zprod.at[pl.ds(0, nz - 1), pl.ds(0, live_rows)])
        sums = place(z_place[...], zprod[...].reshape(nz * SLOT_ROWS, LANES))
        ssend[...] = sums.reshape(ny, ROWS, LANES)
        send_all(Y_SUM, y_peers, lambda p: ssend.at[p], srecv.at[y])
        srecv[y] = ssend[y]

    columns_first = h == 0

    pl.when(columns_first)(slab_vectors)

    wait(recv_sem.at[Y_CODE], ccode.at[pl.ds(0, ny - 1)])
    col_sel = jnp.concatenate(
        [
            onehot(widen(lambda s, p=p: ccode[p, s : s + 1, :]), y * (nz * ROWS))
            for p in range(ny)
        ],
        axis=0,
    )
    wait(recv_sem.at[Z_VEC], vz.at[pl.ds(0, nz - 1)])
    plane = vz[...].reshape(nz * ROWS, TILE)
    picked = jnp.dot(
        col_sel[:, : nz * ROWS].astype(jnp.bfloat16), plane, preferred_element_type=jnp.float32
    )
    for p in range(ny):
        some = picked[SLOT_ROWS * p : SLOT_ROWS * p + live_rows]
        both = jnp.concatenate([some[:, :LANES], some[:, LANES:]], axis=0)
        ysend[p] = both.astype(jnp.bfloat16)
    send_all(Y_VEC, y_peers, lambda p: ysend.at[p], yrecv.at[y])
    yrecv[y] = ysend[y]
    send_all(Z_CODE, z_peers, lambda p: zcode.at[z], zcode.at[z])

    pl.when(jnp.logical_not(columns_first))(slab_vectors)

    wait(recv_sem.at[X_CODE], rcode.at[pl.ds(0, nx - 1)])
    row_place = jnp.concatenate(
        [
            onehot(widen(lambda s, p=p: rcode[p, s : s + 1, :]), x * (nw * ROWS))
            for p in range(nx)
        ],
        axis=0,
    ).T[: nw * ROWS].astype(jnp.bfloat16)
    y_place[...] = col_sel.T[: nz * ROWS].astype(jnp.bfloat16)
    locals_[4].wait()

    pl.when(columns_first)(column_products)

    wait(recv_sem.at[Y_VEC], yrecv.at[pl.ds(0, ny - 1)])
    col_vectors = yrecv[0].astype(jnp.float32)
    for p in range(1, ny):
        col_vectors = col_vectors + yrecv[p].astype(jnp.float32)
    col_vectors = jnp.concatenate([col_vectors[:live_rows], col_vectors[live_rows:]], axis=1)
    rprod[x, 0:live_rows, :] = apply(col_vectors, 1)
    mine_r = rprod.at[x, pl.ds(0, live_rows)]
    send_all(X_PROD, x_peers, lambda p: mine_r, mine_r)

    pl.when(jnp.logical_not(columns_first))(column_products)

    wait(recv_sem.at[Z_CODE], zcode.at[pl.ds(0, nz - 1)])
    z_place[...] = jnp.concatenate(
        [
            onehot(widen(lambda s, p=p: zcode[p, s : s + 1, :]), z * ROWS, (nz - 1) * ROWS)
            for p in range(nz)
        ],
        axis=0,
    ).T[: ny * ROWS].astype(jnp.bfloat16)

    pl.when(columns_first)(column_sums)

    wait(recv_sem.at[X_PROD], rprod.at[pl.ds(0, nx - 1), pl.ds(0, live_rows)])
    sums = place(row_place, rprod[...].reshape(nx * SLOT_ROWS, TILE))
    wsend[...] = sums.reshape(nw, ROWS, TILE)
    send_all(H_PROD, w_peers, lambda p: wsend.at[p], wrecv.at[w])
    wrecv[w] = wsend[w]

    pl.when(jnp.logical_not(columns_first))(column_sums)

    wait(send_sem.at[C_VEC], vx.at[0, pl.ds(0, nc - 1)])
    wait(send_sem.at[H_VEC], vx.at[0, pl.ds(0, nw - nc)])
    wait(send_sem.at[X_CODE], rcode.at[pl.ds(0, nx - 1)])
    wait(send_sem.at[Y_CODE], ccode.at[pl.ds(0, ny - 1)])
    wait(send_sem.at[Z_CODE], zcode.at[pl.ds(0, nz - 1)])
    wait(send_sem.at[Z_VEC], vz.at[pl.ds(0, nz - 1)])
    wait(send_sem.at[X_NEAR], vx.at[pl.ds(0, nx - 1), pl.ds(0, nc)])
    wait(send_sem.at[X_FAR], vx.at[pl.ds(0, nx - 1), pl.ds(0, nw - nc)])
    wait(send_sem.at[Y_VEC], ysend.at[pl.ds(0, ny - 1)])
    wait(send_sem.at[Y_PROD], yprod.at[pl.ds(0, ny - 1), pl.ds(0, live_rows)])
    wait(send_sem.at[Z_PROD], zprod.at[pl.ds(0, nz - 1), pl.ds(0, live_rows)])
    wait(send_sem.at[X_PROD], rprod.at[pl.ds(0, nx - 1), pl.ds(0, live_rows)])

    wait(recv_sem.at[Y_SUM], srecv.at[pl.ds(0, ny - 1)])
    right = srecv[0]
    for p in range(1, ny):
        right = right + srecv[p]
    wait(recv_sem.at[Z_SUM], zrecv.at[pl.ds(0, nz - 1)])
    left = zrecv[0]
    for p in range(1, nz):
        left = left + zrecv[p]
    total = jnp.concatenate([left, right], axis=1)
    wait(send_sem.at[Z_SUM], zsend.at[pl.ds(0, nz - 1)])
    wait(send_sem.at[Y_SUM], ssend.at[pl.ds(0, ny - 1)])
    wait(send_sem.at[H_PROD], wsend.at[pl.ds(0, nw - 1)])
    wait(recv_sem.at[H_PROD], wrecv.at[pl.ds(0, nw - 1)])
    for p in range(nw):
        total = total + wrecv[p]
    for j in range(VB):
        out_ref[j] = total[NVEC * j : NVEC * (j + 1), :]


def on_device(sizes, vectors, tiles, tile_rows, tile_cols, tile_counts):
    ny, nz, nx, nh, nc = sizes
    nw = nh * nc
    live_rows = tiles.shape[2] * NVEC
    bf16, f32, i32 = jnp.bfloat16, jnp.float32, jnp.int32
    vmem, smem = pltpu.VMEM, pltpu.SMEM
    return pl.pallas_call(
        functools.partial(kernel, sizes),
        out_shape=pltpu.VMEM(vectors.shape, f32),
        in_specs=[pl.BlockSpec(memory_space=pltpu.HBM)] * 5,
        out_specs=pl.BlockSpec(memory_space=pltpu.VMEM),
        scratch_shapes=[
            vmem(vectors.shape, bf16),
            vmem(tiles.shape[2:], bf16),
            smem(tile_rows.shape, i32),
            smem(tile_cols.shape, i32),
            smem(tile_counts.shape, i32),
            vmem((nz, ROWS, TILE), bf16),
            vmem((nx, nw, ROWS, TILE), bf16),
            vmem((ny, PAD, LANES), i32),
            vmem((nz, PAD, LANES), i32),
            vmem((nx, PAD, LANES), i32),
            vmem((ny, 2 * live_rows, LANES), bf16),
            vmem((ny, 2 * live_rows, LANES), bf16),
            vmem((ny, SLOT_ROWS, LANES), f32),
            vmem((nz, SLOT_ROWS, LANES), f32),
            vmem((nx, SLOT_ROWS, TILE), f32),
            vmem((nz, ROWS, LANES), f32),
            vmem((nz, ROWS, LANES), f32),
            vmem((ny, ROWS, LANES), f32),
            vmem((ny, ROWS, LANES), f32),
            vmem((nw, ROWS, TILE), f32),
            vmem((nw, ROWS, TILE), f32),
            vmem((nz * ROWS, ny * SLOT_ROWS), bf16),
            vmem((ny * ROWS, nz * SLOT_ROWS), bf16),
            pltpu.SemaphoreType.DMA((5,)),
            pltpu.SemaphoreType.DMA((GROUPS,)),
            pltpu.SemaphoreType.DMA((GROUPS,)),
        ],
        compiler_params=pltpu.CompilerParams(
            collective_id=0, has_side_effects=True, vmem_limit_bytes=60 * 2**20
        ),
        cost_estimate=pl.CostEstimate(
            flops=2**24, bytes_accessed=2**20, transcendentals=0
        ),
    )(vectors, tiles, tile_rows, tile_cols, tile_counts)


def build(mesh, nz, nh, nc):
    ny, nx = mesh.shape["row"] // nz, mesh.shape["col"] // (nh * nc)
    placed = (
        P(("row", "col"), None, None),
        P("row", "col", None, None, None),
        P("row", "col", None),
        P("row", "col", None),
        P("row", "col"),
    )
    return jax.shard_map(
        functools.partial(on_device, (ny, nz, nx, nh, nc)),
        mesh=mesh,
        in_specs=placed,
        out_specs=P(("row", "col"), None, None),
        check_vma=False,
    )


def solution(mesh):
    return build(mesh, 8, 2, 2)
```

```python
import functools

import jax
import jax.numpy as jnp
from jax import lax
from jax.experimental import pallas as pl
from jax.experimental.pallas import tpu as pltpu
from jax.sharding import PartitionSpec as P

MESH = pl.DeviceIdType.MESH
NVEC = 4
TILE = 256
VB = 4
ROWS = VB * NVEC
PAD = 8
SLOT_ROWS = PAD * NVEC
LANES = 128
NONE = -(2**20)

GROUPS = 17
C_VEC, H_VEC, D_VEC, X_CODE, Y_CODE, Z_CODE, Z_VEC, X_NEAR, X_FAR, X_DIAG, Y_VEC = range(11)
Y_PROD, Z_SUM, Z_PROD, Y_SUM, X_PROD, H_PROD = range(11, GROUPS)


def widen(row_of):
    sub = lax.broadcasted_iota(jnp.int32, (8, LANES), 0)
    pieces = []
    for k in range(PAD // 2):
        low = jnp.broadcast_to(row_of(2 * k), (8, LANES))
        high = jnp.broadcast_to(row_of(2 * k + 1), (8, LANES))
        pieces.append(jnp.where(sub < 4, low, high) + (sub & 3))
    return jnp.concatenate(pieces, axis=0)


def onehot(codes, base, gap=0):
    lane = lax.broadcasted_iota(jnp.int32, codes.shape, 1)
    target = lane + base + (lane // ROWS) * gap
    return jnp.where(codes == target, 1.0, 0.0).astype(jnp.float32)


def place(matrix, products):
    high = products.astype(jnp.bfloat16)
    low = (products - high.astype(jnp.float32)).astype(jnp.bfloat16)
    return jnp.dot(matrix, high, preferred_element_type=jnp.float32) + jnp.dot(
        matrix, low, preferred_element_type=jnp.float32
    )


def kernel(
    sizes,
    vec_hbm, tiles_hbm, rows_hbm, cols_hbm, counts_hbm,
    out_ref,
    vin, tiles, rows_s, cols_s, counts_s,
    vz, vx, ccode, zcode, rcode, ysend, yrecv, yprod, zprod, rprod,
    zsend, zrecv, ssend, srecv, wsend, wrecv, y_place, z_place,
    local_sem, send_sem, recv_sem,
):
    ny, nz, nx, nh, nc = sizes
    nw = nh * nc
    slots = tiles.shape[0]
    live_rows = slots * NVEC
    row, col = lax.axis_index("row"), lax.axis_index("col")
    y, z = row // nz, row % nz
    x, w = col // nw, col % nw
    h = w // nc

    def at(y_, z_, x_, w_):
        return (y_ * nz + z_, x_ * nw + w_)

    def peers(me, n, place_of, line=False):
        out = []
        for k in sorted(range(1, n), key=lambda k: min(k, n - k) * (1 if line else -1)):
            p = lax.rem(me + k, n)
            out.append((p, place_of(p)))
        return out

    y_peers = peers(y, ny, lambda p: at(p, z, x, w))
    z_peers = peers(z, nz, lambda p: at(y, p, x, w), line=True)
    x_peers = peers(x, nx, lambda p: at(y, z, p, w))
    cores = [h * nc + lax.rem(w + k, nc) for k in range(nc)]
    core_peers = [(p, at(y, z, x, p)) for p in cores[1:]]
    far_peers = [(p, at(y, z, x, p)) for p in [nw - nc - h * nc + (c - h * nc) for c in cores]]
    w_peers = far_peers[::-1] + core_peers

    locals_ = [
        pltpu.make_async_copy(src, dst, local_sem.at[i])
        for i, (src, dst) in enumerate(
            (
                (vec_hbm, vin),
                (rows_hbm, rows_s),
                (cols_hbm, cols_s),
                (counts_hbm, counts_s),
                (tiles_hbm.at[0, 0], tiles),
            )
        )
    ]
    locals_[0].start()
    barrier = pltpu.get_barrier_semaphore()
    ordered = w_peers[:1] + y_peers[:3] + z_peers[:5] + w_peers[1:] + y_peers[3:] + x_peers + z_peers[5:]
    everyone = [device_id for _, device_id in ordered]
    for device_id in everyone:
        pl.semaphore_signal(barrier, inc=1, device_id=device_id, device_id_type=MESH)
    for copy in locals_[1:]:
        copy.start()

    def send(which, src, dst, device_id):
        pltpu.make_async_remote_copy(
            src_ref=src,
            dst_ref=dst,
            send_sem=send_sem.at[which],
            recv_sem=recv_sem.at[which],
            device_id=device_id,
            device_id_type=MESH,
        ).start()

    def wait(sem, ref):
        pltpu.make_async_copy(ref, ref, sem).wait()

    def send_all(which, peers_, src_of, dst):
        for p, device_id in peers_:
            send(which, src_of(p), dst, device_id)

    tail = SLOT_ROWS - live_rows
    if tail:
        yprod[:, live_rows:, :] = jnp.zeros((ny, tail, LANES), jnp.float32)
        zprod[:, live_rows:, :] = jnp.zeros((nz, tail, LANES), jnp.float32)
        rprod[:, live_rows:, :] = jnp.zeros((nx, tail, TILE), jnp.float32)

    locals_[0].wait()
    own = jnp.concatenate([vin[j].astype(jnp.float32) for j in range(VB)], axis=0)
    own = own.astype(jnp.bfloat16)
    vz[z] = own
    vx[x, w] = own
    for i in (1, 2, 3):
        locals_[i].wait()
    live = counts_s[0, 0]
    sub = lax.broadcasted_iota(jnp.int32, (PAD, LANES), 0)
    col_codes = jnp.full((PAD, LANES), NONE, jnp.int32)
    row_codes = col_codes
    for s in range(slots):
        q = cols_s[0, 0, s] * NVEC
        p = rows_s[0, 0, s] * NVEC
        col_codes = jnp.where(sub == s, jnp.where(s < live, q, NONE), col_codes)
        row_codes = jnp.where(sub == s, jnp.where(s < live, p, NONE), row_codes)
    ccode[y] = col_codes
    zcode[z] = col_codes
    rcode[x] = row_codes

    own_row_codes = widen(lambda s: row_codes[s : s + 1, :])
    slab_rows = nx * nw * ROWS
    pieces = [
        onehot(own_row_codes, b)[:, : min(LANES, slab_rows - b)]
        for b in range(0, slab_rows, LANES)
    ]
    row_sel = jnp.concatenate(pieces, axis=1).astype(jnp.bfloat16)
    half = lax.broadcasted_iota(jnp.int32, (8, TILE), 0) < 4

    def apply(vectors, contract):
        outs = []
        for k in range((slots + 1) // 2):
            pair = vectors[8 * k : 8 * k + 8].astype(jnp.bfloat16)
            both = [
                lax.dot_general(
                    pair,
                    tiles[min(2 * k + i, slots - 1)],
                    (((1,), (contract,)), ((), ())),
                    preferred_element_type=jnp.float32,
                )
                for i in range(2)
            ]
            outs.append(jnp.where(half, both[0], both[1]))
        return jnp.concatenate(outs, axis=0)[:live_rows]

    pl.semaphore_wait(barrier, len(everyone))

    send_all(D_VEC, far_peers[1:], lambda p: vx.at[x, w], vx.at[x, w])
    send_all(H_VEC, far_peers[:1], lambda p: vx.at[x, w], vx.at[x, w])
    send_all(C_VEC, core_peers, lambda p: vx.at[x, w], vx.at[x, w])
    send_all(Z_VEC, z_peers, lambda p: vz.at[z], vz.at[z])
    send_all(Y_CODE, y_peers, lambda p: ccode.at[y], ccode.at[y])
    send_all(X_CODE, x_peers, lambda p: rcode.at[x], rcode.at[x])

    def slab_vectors():
        wait(recv_sem.at[C_VEC], vx.at[0, pl.ds(0, nc - 1)])
        near = vx.at[x, pl.ds(h * nc, nc)]
        send_all(X_NEAR, x_peers, lambda p: near, near)
        for arrived, onward, (p, _) in zip((H_VEC, D_VEC), (X_FAR, X_DIAG), far_peers):
            wait(recv_sem.at[arrived], vx.at[0, 0])
            far = vx.at[x, p]
            send_all(onward, x_peers, lambda p: far, far)

    def column_products():
        wait(recv_sem.at[X_NEAR], vx.at[pl.ds(0, nx - 1), pl.ds(0, nc)])
        wait(recv_sem.at[X_FAR], vx.at[pl.ds(0, nx - 1), 0])
        wait(recv_sem.at[X_DIAG], vx.at[pl.ds(0, nx - 1), 0])
        row_vectors = jnp.dot(
            row_sel, vx[...].reshape(slab_rows, TILE), preferred_element_type=jnp.float32
        )
        products = apply(row_vectors, 0)
        zprod[z, 0:live_rows, :] = products[:, LANES:]
        mine_z = zprod.at[z, pl.ds(0, live_rows)]
        send_all(Z_PROD, z_peers, lambda p: mine_z, mine_z)
        yprod[y, 0:live_rows, :] = products[:, :LANES]
        mine_y = yprod.at[y, pl.ds(0, live_rows)]
        send_all(Y_PROD, y_peers, lambda p: mine_y, mine_y)

    def column_sums():
        wait(recv_sem.at[Y_PROD], yprod.at[pl.ds(0, ny - 1), pl.ds(0, live_rows)])
        sums = place(y_place[...], yprod[...].reshape(ny * SLOT_ROWS, LANES))
        zsend[...] = sums.reshape(nz, ROWS, LANES)
        send_all(Z_SUM, z_peers, lambda p: zsend.at[p], zrecv.at[z])
        zrecv[z] = zsend[z]
        wait(recv_sem.at[Z_PROD], zprod.at[pl.ds(0, nz - 1), pl.ds(0, live_rows)])
        sums = place(z_place[...], zprod[...].reshape(nz * SLOT_ROWS, LANES))
        ssend[...] = sums.reshape(ny, ROWS, LANES)
        send_all(Y_SUM, y_peers, lambda p: ssend.at[p], srecv.at[y])
        srecv[y] = ssend[y]

    columns_first = h == 0

    pl.when(columns_first)(slab_vectors)

    wait(recv_sem.at[Y_CODE], ccode.at[pl.ds(0, ny - 1)])
    col_sel = jnp.concatenate(
        [
            onehot(widen(lambda s, p=p: ccode[p, s : s + 1, :]), y * (nz * ROWS))
            for p in range(ny)
        ],
        axis=0,
    )
    wait(recv_sem.at[Z_VEC], vz.at[pl.ds(0, nz - 1)])
    plane = vz[...].reshape(nz * ROWS, TILE)
    picked = jnp.dot(
        col_sel[:, : nz * ROWS].astype(jnp.bfloat16), plane, preferred_element_type=jnp.float32
    )
    for p in range(ny):
        some = picked[SLOT_ROWS * p : SLOT_ROWS * p + live_rows]
        both = jnp.concatenate([some[:, :LANES], some[:, LANES:]], axis=0)
        ysend[p] = both.astype(jnp.bfloat16)
    send_all(Y_VEC, y_peers, lambda p: ysend.at[p], yrecv.at[y])
    yrecv[y] = ysend[y]
    send_all(Z_CODE, z_peers, lambda p: zcode.at[z], zcode.at[z])

    pl.when(jnp.logical_not(columns_first))(slab_vectors)

    wait(recv_sem.at[X_CODE], rcode.at[pl.ds(0, nx - 1)])
    row_place = jnp.concatenate(
        [
            onehot(widen(lambda s, p=p: rcode[p, s : s + 1, :]), x * (nw * ROWS))
            for p in range(nx)
        ],
        axis=0,
    ).T[: nw * ROWS].astype(jnp.bfloat16)
    y_place[...] = col_sel.T[: nz * ROWS].astype(jnp.bfloat16)
    locals_[4].wait()

    pl.when(columns_first)(column_products)

    wait(recv_sem.at[Y_VEC], yrecv.at[pl.ds(0, ny - 1)])
    col_vectors = yrecv[0].astype(jnp.float32)
    for p in range(1, ny):
        col_vectors = col_vectors + yrecv[p].astype(jnp.float32)
    col_vectors = jnp.concatenate([col_vectors[:live_rows], col_vectors[live_rows:]], axis=1)
    rprod[x, 0:live_rows, :] = apply(col_vectors, 1)
    mine_r = rprod.at[x, pl.ds(0, live_rows)]
    send_all(X_PROD, x_peers, lambda p: mine_r, mine_r)

    pl.when(jnp.logical_not(columns_first))(column_products)

    wait(recv_sem.at[Z_CODE], zcode.at[pl.ds(0, nz - 1)])
    z_place[...] = jnp.concatenate(
        [
            onehot(widen(lambda s, p=p: zcode[p, s : s + 1, :]), z * ROWS, (nz - 1) * ROWS)
            for p in range(nz)
        ],
        axis=0,
    ).T[: ny * ROWS].astype(jnp.bfloat16)

    pl.when(columns_first)(column_sums)

    wait(recv_sem.at[X_PROD], rprod.at[pl.ds(0, nx - 1), pl.ds(0, live_rows)])
    sums = place(row_place, rprod[...].reshape(nx * SLOT_ROWS, TILE))
    wsend[...] = sums.reshape(nw, ROWS, TILE)
    send_all(H_PROD, w_peers, lambda p: wsend.at[p], wrecv.at[w])
    wrecv[w] = wsend[w]

    pl.when(jnp.logical_not(columns_first))(column_sums)

    wait(send_sem.at[C_VEC], vx.at[0, pl.ds(0, nc - 1)])
    wait(send_sem.at[H_VEC], vx.at[0, 0])
    wait(send_sem.at[D_VEC], vx.at[0, 0])
    wait(send_sem.at[X_CODE], rcode.at[pl.ds(0, nx - 1)])
    wait(send_sem.at[Y_CODE], ccode.at[pl.ds(0, ny - 1)])
    wait(send_sem.at[Z_CODE], zcode.at[pl.ds(0, nz - 1)])
    wait(send_sem.at[Z_VEC], vz.at[pl.ds(0, nz - 1)])
    wait(send_sem.at[X_NEAR], vx.at[pl.ds(0, nx - 1), pl.ds(0, nc)])
    wait(send_sem.at[X_FAR], vx.at[pl.ds(0, nx - 1), 0])
    wait(send_sem.at[X_DIAG], vx.at[pl.ds(0, nx - 1), 0])
    wait(send_sem.at[Y_VEC], ysend.at[pl.ds(0, ny - 1)])
    wait(send_sem.at[Y_PROD], yprod.at[pl.ds(0, ny - 1), pl.ds(0, live_rows)])
    wait(send_sem.at[Z_PROD], zprod.at[pl.ds(0, nz - 1), pl.ds(0, live_rows)])
    wait(send_sem.at[X_PROD], rprod.at[pl.ds(0, nx - 1), pl.ds(0, live_rows)])

    wait(recv_sem.at[Y_SUM], srecv.at[pl.ds(0, ny - 1)])
    right = srecv[0]
    for p in range(1, ny):
        right = right + srecv[p]
    wait(recv_sem.at[Z_SUM], zrecv.at[pl.ds(0, nz - 1)])
    left = zrecv[0]
    for p in range(1, nz):
        left = left + zrecv[p]
    total = jnp.concatenate([left, right], axis=1)
    wait(send_sem.at[Z_SUM], zsend.at[pl.ds(0, nz - 1)])
    wait(send_sem.at[Y_SUM], ssend.at[pl.ds(0, ny - 1)])
    wait(send_sem.at[H_PROD], wsend.at[pl.ds(0, nw - 1)])
    wait(recv_sem.at[H_PROD], wrecv.at[pl.ds(0, nw - 1)])
    for p in range(nw):
        total = total + wrecv[p]
    for j in range(VB):
        out_ref[j] = total[NVEC * j : NVEC * (j + 1), :]


def on_device(sizes, vectors, tiles, tile_rows, tile_cols, tile_counts):
    ny, nz, nx, nh, nc = sizes
    nw = nh * nc
    live_rows = tiles.shape[2] * NVEC
    bf16, f32, i32 = jnp.bfloat16, jnp.float32, jnp.int32
    vmem, smem = pltpu.VMEM, pltpu.SMEM
    return pl.pallas_call(
        functools.partial(kernel, sizes),
        out_shape=pltpu.VMEM(vectors.shape, f32),
        in_specs=[pl.BlockSpec(memory_space=pltpu.HBM)] * 5,
        out_specs=pl.BlockSpec(memory_space=pltpu.VMEM),
        scratch_shapes=[
            vmem(vectors.shape, bf16),
            vmem(tiles.shape[2:], bf16),
            smem(tile_rows.shape, i32),
            smem(tile_cols.shape, i32),
            smem(tile_counts.shape, i32),
            vmem((nz, ROWS, TILE), bf16),
            vmem((nx, nw, ROWS, TILE), bf16),
            vmem((ny, PAD, LANES), i32),
            vmem((nz, PAD, LANES), i32),
            vmem((nx, PAD, LANES), i32),
            vmem((ny, 2 * live_rows, LANES), bf16),
            vmem((ny, 2 * live_rows, LANES), bf16),
            vmem((ny, SLOT_ROWS, LANES), f32),
            vmem((nz, SLOT_ROWS, LANES), f32),
            vmem((nx, SLOT_ROWS, TILE), f32),
            vmem((nz, ROWS, LANES), f32),
            vmem((nz, ROWS, LANES), f32),
            vmem((ny, ROWS, LANES), f32),
            vmem((ny, ROWS, LANES), f32),
            vmem((nw, ROWS, TILE), f32),
            vmem((nw, ROWS, TILE), f32),
            vmem((nz * ROWS, ny * SLOT_ROWS), bf16),
            vmem((ny * ROWS, nz * SLOT_ROWS), bf16),
            pltpu.SemaphoreType.DMA((5,)),
            pltpu.SemaphoreType.DMA((GROUPS,)),
            pltpu.SemaphoreType.DMA((GROUPS,)),
        ],
        compiler_params=pltpu.CompilerParams(
            collective_id=0, has_side_effects=True, vmem_limit_bytes=60 * 2**20
        ),
        cost_estimate=pl.CostEstimate(
            flops=2**24, bytes_accessed=2**20, transcendentals=0
        ),
    )(vectors, tiles, tile_rows, tile_cols, tile_counts)


def build(mesh, nz, nh, nc):
    ny, nx = mesh.shape["row"] // nz, mesh.shape["col"] // (nh * nc)
    placed = (
        P(("row", "col"), None, None),
        P("row", "col", None, None, None),
        P("row", "col", None),
        P("row", "col", None),
        P("row", "col"),
    )
    return jax.shard_map(
        functools.partial(on_device, (ny, nz, nx, nh, nc)),
        mesh=mesh,
        in_specs=placed,
        out_specs=P(("row", "col"), None, None),
        check_vma=False,
    )


def solution(mesh):
    return build(mesh, 8, 2, 2)
```
